32 devices in a mesh: grp: 1, dap: 16 (over z, y, x), sub: 2 (over core).
Axes of the slice: x: 2, y: 2, z: 4, core: 2. Of those that a mesh axis runs over, the one named last changes fastest.
Arguments:
- pair_state: bfloat16 [384, 384, 128], P(('grp', 'dap', 'sub')), may hold values from -6 to 6
- residue_mask: int32 [384], P('grp'), may hold values 0 or 1
- norm_gain: float32 [2, 128], replicated, may hold values from 0.5 to 1.5
- edge_weight: bfloat16 [2, 128, 512], replicated, may hold values from -0.5 to 0.5
- gate_weight: bfloat16 [2, 128, 128], replicated, may hold values from -0.5 to 0.5
- out_weight: bfloat16 [2, 128, 128], replicated, may hold values from -0.5 to 0.5
- mix_gain: float32 [2, 128], replicated, may hold values from 0.5 to 1.5
Outputs:
- updated: bfloat16 [384, 384, 128], P(('grp', 'dap', 'sub'))
The draws below stay inside these ranges and needn't reach their ends.
All inputs are finite; a program needn't handle non-finite values.
Results may differ from the reference program's by a relative error of at most 0.0075.
Values may be sent and summed in bfloat16 or wider, within the bound.
A program may use at most 64 MiB of HBM per device.

```python
import jax
import jax.numpy as jnp
from jax import lax

C = 128
HID = 128
N = 384


def touch_ends(values, key, low, top_value):
    shape = values.shape
    spot = [jax.random.randint(jax.random.fold_in(key, axis), (), 0, shape[axis]) for axis in range(len(shape))]
    values = values.at[tuple(spot)].set(low)
    longest = shape.index(max(shape))
    spot[longest] = (spot[longest] + 1) % shape[longest]
    return values.at[tuple(spot)].set(top_value)


def level_of(own_key, dims, split, smallest, top_value):
    loudness = 1.0
    for dim, blocks in split:
        draws = jax.random.uniform(jax.random.fold_in(jax.random.fold_in(own_key, 6), dim), (blocks,), jnp.float32, smallest / len(split), top_value / len(split))
        loudness = loudness * jnp.repeat(jnp.exp(draws), dims[dim] // blocks).reshape((-1,) + (1,) * (len(dims) - 1 - dim))
    return loudness


def noise(rng, extent, width, reach, cuts=(), held_as=jnp.bfloat16):
    drawn = width * jax.random.normal(rng, extent, jnp.float32)
    if cuts:
        drawn = drawn * level_of(rng, extent, cuts, -0.22, 0.18)
    return jnp.clip(drawn, -reach, reach).astype(held_as)


def setup_inputs(seed: int = 0, part: int = 0) -> dict:
    streams_of = jax.random.split(jax.random.key(seed), 8)
    part_keys = jax.random.split(jax.random.fold_in(streams_of[7], part), 8)
    return {
        "pair_state": noise(part_keys[0], (N, N, C), 1.0, 6.0, ((0, 32),)),
        "residue_mask": touch_ends((jax.random.randint(part_keys[1], (N,), 0, 8) < 7).astype(jnp.int32), jax.random.fold_in(part_keys[1], 1), 0, 1),
        "norm_gain": jnp.clip(jax.random.uniform(streams_of[2], (2, C), jnp.float32, 0.5, 1.5), 0.5, 1.5),
        "edge_weight": noise(streams_of[3], (2, C, 4 * HID), C ** -0.5, 0.5),
        "gate_weight": noise(streams_of[4], (2, C, C), C ** -0.5, 0.5),
        "out_weight": noise(streams_of[5], (2, HID, C), HID ** -0.5, 0.5),
        "mix_gain": jnp.clip(jax.random.uniform(streams_of[6], (2, HID), jnp.float32, 0.5, 1.5), 0.5, 1.5),
    }


def layer_norm(values, gain, axis):
    average = lax.optimization_barrier(jnp.mean(values, axis=axis, keepdims=True))
    centered = values - average
    variance = lax.optimization_barrier(jnp.mean(centered * centered, axis=axis, keepdims=True))
    return centered * lax.rsqrt(variance + 1e-05) * gain

def reference(pair_state, residue_mask, norm_gain, edge_weight, gate_weight, out_weight, mix_gain):
    mask_values = residue_mask.astype(jnp.float32)
    pair_mask = mask_values[:, None] * mask_values[None, :]
    hidden = out_weight.shape[1]
    current = pair_state
    for layer_index in range(2):
        values = current.astype(jnp.float32)
        normed = layer_norm(values, norm_gain[layer_index], -1).astype(jnp.bfloat16)
        normed_wide = normed.astype(jnp.float32)
        weights = edge_weight[layer_index].astype(jnp.float32)
        left_val = jnp.einsum('rnc,cf->frn', normed_wide, weights[:, :hidden])
        left_gate = jnp.einsum('rnc,cf->frn', normed_wide, weights[:, hidden:2 * hidden])
        left_side = (jax.nn.sigmoid(left_gate) * left_val * pair_mask).astype(jnp.bfloat16)
        right_val = jnp.einsum('rnc,cf->frn', normed_wide, weights[:, 2 * hidden:3 * hidden])
        right_gate = jnp.einsum('rnc,cf->frn', normed_wide, weights[:, 3 * hidden:])
        right_side = (jax.nn.sigmoid(right_gate) * right_val * pair_mask).astype(jnp.bfloat16)
        gating = jax.nn.sigmoid(jnp.einsum('rnc,cd->rnd', normed_wide, gate_weight[layer_index].astype(jnp.float32)))
        left_wide = left_side.astype(jnp.float32)
        right_wide = right_side.astype(jnp.float32)
        if layer_index == 0:
            mixed = jnp.einsum('hik,hjk->hij', left_wide, right_wide)
        else:
            mixed = jnp.einsum('hki,hkj->hij', left_wide, right_wide)
        mixed = mixed.astype(jnp.bfloat16)
        normed_mix = layer_norm(mixed.astype(jnp.float32), mix_gain[layer_index][:, None, None], 0).astype(jnp.bfloat16)
        update = jnp.einsum('hrn,hc->rnc', normed_mix.astype(jnp.float32), out_weight[layer_index].astype(jnp.float32))
        current = (values + gating * update).astype(jnp.bfloat16)
    return current
```

```python
import functools

import jax
import jax.numpy as jnp
from jax import lax
from jax.experimental import pallas as pl
from jax.experimental.pallas import tpu as pltpu
from jax.sharding import PartitionSpec as P

PER = 8
GROUP = 4
CHUNKS = 2
LANES = 128
TILE = 16
F32 = jnp.float32
BF16 = jnp.bfloat16


def sigmoid(x):
    return 0.5 * jnp.tanh(0.5 * x) + 0.5


def kernel(
    n, n_sub,
    z_ref, mask_s, mask_v, ng_ref, ew_ref, gw_ref, ow_ref, mg_ref,
    out_ref,
    wt, normed, send_l, send_r, recv_l, recv_r, stage, lh, rh, mf, send_m, recv_m,
    ss_l, ss_r, ss_m, rs_l, rs_r, rs_m,
):
    rows, cols, _ = z_ref.shape
    hidden = ow_ref.shape[1]
    owners = hidden // PER
    splits = n // owners
    block = rows * PER
    pairs = rows // 2
    pairs_chunk = pairs // CHUNKS
    span = pairs_chunk * TILE
    width = mf.shape[0] * LANES
    part = owners * rows

    me = lax.axis_index("dap") * n_sub + lax.axis_index("sub")
    split = lax.div(me, owners)
    mine = lax.rem(me, owners)
    first = split * owners

    def device(p):
        return {"dap": lax.div(p, n_sub), "sub": lax.rem(p, n_sub)}

    def loop(lo, hi, body):
        lax.fori_loop(lo, hi, lambda i, c: (body(i), c)[1], 0)

    barrier = pltpu.get_barrier_semaphore()
    loop(1, n, lambda k: pl.semaphore_signal(
        barrier, inc=1, device_id=device(lax.rem(me + k, n)),
        device_id_type=pl.DeviceIdType.MESH))

    def remote(src, dst, ssem, rsem, p):
        return pltpu.make_async_remote_copy(
            src_ref=src, dst_ref=dst, send_sem=ssem, recv_sem=rsem,
            device_id=device(p), device_id_type=pl.DeviceIdType.MESH)

    def left_copy(c, q):
        at = pl.ds(c * span, span)
        return remote(send_l.at[q, at], recv_l.at[mine, at], ss_l.at[c, q], rs_l.at[c, mine], first + q)

    def left_from(c, q):
        at = pl.ds(c * span, span)
        return remote(send_l.at[q, at], recv_l.at[q, at], ss_l.at[c, q], rs_l.at[c, q], first + q)

    def right_copy(c, p):
        at = pl.ds(c * span, span)
        return remote(send_r.at[lax.rem(p, owners), at], recv_r.at[me, at], ss_r.at[c, p], rs_r.at[c, me], p)

    def right_from(c, p):
        at = pl.ds(c * span, span)
        return remote(send_r.at[lax.rem(p, owners), at], recv_r.at[p, at], ss_r.at[c, p], rs_r.at[c, p], p)

    def mix_copy(q, p):
        return remote(send_m.at[q], recv_m.at[me], ss_m.at[p], rs_m.at[me], p)

    def mix_from(q, p):
        return remote(send_m.at[q], recv_m.at[p], ss_m.at[p], rs_m.at[p], p)

    columns = mask_v[...].astype(F32)

    def start_chunk(t, c):
        at = pl.ds(c * span, span)
        recv_l[mine, at] = send_l[mine, at]
        recv_r[me, at] = send_r[mine, at]

        if t == 0:
            def far(k):
                @pl.when(lax.div(lax.rem(me + k, n), owners) != split)
                def _():
                    right_copy(c, lax.rem(me + k, n)).start()
            loop(1, n, far)

        def near(k):
            q = lax.rem(mine + k, owners)
            right_copy(c, first + q).start()
            left_copy(c, q).start()
        loop(1, owners, near)

    def project(t, u, values_pair):
        sides = []
        for i in range(2):
            r = 2 * u + i
            values = values_pair[i]
            mean = jnp.mean(values, axis=-1, keepdims=True)
            centered = values - mean
            var = jnp.mean(centered * centered, axis=-1, keepdims=True)
            nr = (centered * lax.rsqrt(var + 1e-05) * ng_ref[pl.ds(t, 1), :]).astype(BF16)
            normed[r] = nr
            proj = lax.dot_general(wt[...], nr, (((1,), (1,)), ((), ())), preferred_element_type=F32)
            mask = columns * mask_s[me * rows + r].astype(F32)
            sides.append((
                sigmoid(proj[hidden:2 * hidden]) * proj[:hidden] * mask,
                sigmoid(proj[3 * hidden:]) * proj[2 * hidden:3 * hidden] * mask,
            ))
        at = pl.ds(pl.multiple_of(u * TILE, TILE), TILE)
        for ref, k in ((send_l, 0), (send_r, 1)):
            both = jnp.concatenate(
                [sides[i][k].reshape(owners, PER, cols) for i in range(2)], axis=1)
            ref[:, at, :] = both.astype(BF16)

    def finish(t, u, z):
        at = pl.ds(pl.multiple_of(u * TILE, TILE), TILE)
        if t == 0:
            got = recv_m[pl.ds(first, owners), at, :].astype(F32)
        else:
            got = recv_m[pl.ds(0, owners), at, :].astype(F32)
            for s in range(1, splits):
                got = got + recv_m[pl.ds(s * owners, owners), at, :].astype(F32)
        result = []
        for i in range(2):
            r = 2 * u + i
            mixed = got[:, i * PER:(i + 1) * PER, :].reshape(hidden, cols)
            mean = jnp.mean(mixed, axis=0, keepdims=True)
            centered = mixed - mean
            var = jnp.mean(centered * centered, axis=0, keepdims=True)
            nm = (centered * lax.rsqrt(var + 1e-05) * mg_ref[t]).astype(BF16)
            update = lax.dot_general(nm, ow_ref[t], (((0,), (0,)), ((), ())), preferred_element_type=F32)
            gate = sigmoid(jnp.dot(normed[r], gw_ref[t], preferred_element_type=F32))
            new = (z[r].astype(F32) + gate * update).astype(BF16)
            out_ref[r] = new
            result.append(new.astype(F32))
        return result

    def sort(src, base, dst, at, g):
        for v in range(cols // LANES):
            lanes = pl.ds(v * LANES, LANES)
            stage[v] = src[pl.ds(base + g * GROUP, GROUP), :, lanes].astype(F32).reshape(stage.shape[1:])
            for h in range(PER):
                dst[h, pl.ds(pl.multiple_of(at + g * GROUP * rows, TILE), GROUP * rows), lanes] = stage[
                    v, pl.ds(h, GROUP * rows, stride=PER), :].astype(BF16)

    def spread(h, count, product):
        for v in range(width // LANES):
            mf[v, pl.ds(h, count, stride=PER), :] = product[:, v * LANES:(v + 1) * LANES]

    def gather(slot, q, jc):
        for v in range(width // LANES):
            send_m[slot, :, pl.ds(jc * width + v * LANES, LANES)] = mf[
                v, pl.ds(pl.multiple_of(q * block, TILE), block), :].astype(BF16)

    def wait_left(g):
        def one(q):
            @pl.when(q != mine)
            def _():
                for c in range(CHUNKS):
                    left_from(c, q).wait_recv()
        loop(g * GROUP, (g + 1) * GROUP, one)

    def wait_right(base, g):
        def one(p):
            @pl.when(p != me)
            def _():
                for c in range(CHUNKS):
                    right_from(c, p).wait_recv()
        loop(base + g * GROUP, base + (g + 1) * GROUP, one)

    def prepare(t):
        wt[...] = ew_ref[t].astype(F32).T.astype(BF16)

    def project_all(t):
        for c in range(CHUNKS):
            def body(u):
                if t == 0:
                    project(t, u, [z_ref[2 * u].astype(F32), z_ref[2 * u + 1].astype(F32)])
                else:
                    project(t, u, finish(0, u, z_ref))
            loop(c * pairs_chunk, (c + 1) * pairs_chunk, body)
            if t == 0 and c == 0:
                pl.semaphore_wait(barrier, n - 1)
            start_chunk(t, c)

    def wait_sent(t):
        def one(p):
            @pl.when(p != me)
            def _():
                for c in range(CHUNKS):
                    right_from(c, p).wait_send()
        if t == 0:
            loop(0, n, one)
        else:
            loop(first, first + owners, one)

        def two(q):
            @pl.when(q != mine)
            def _():
                for c in range(CHUNKS):
                    left_from(c, q).wait_send()
        loop(0, owners, two)

    prepare(0)
    project_all(0)
    prepare(1)

    def left_in(g):
        wait_left(g)
        sort(recv_l, 0, lh, 0, g)
    loop(0, owners // GROUP, left_in)

    for jc in range(cols // width):
        sources = width // rows

        def right_in(g):
            wait_right(jc * sources, g)
            sort(recv_r, jc * sources, rh, 0, g)
        loop(0, sources // GROUP, right_in)
        for h in range(PER):
            spread(h, part, lax.dot_general(
                lh[h], rh[h], (((1,), (1,)), ((), ())), preferred_element_type=F32))
        loop(0, owners, lambda q: gather(q, q, jc))

    recv_m[me] = send_m[mine]
    loop(1, owners, lambda k: mix_copy(
        lax.rem(mine + k, owners), first + lax.rem(mine + k, owners)).start())
    wait_sent(0)

    def mix_in(p):
        @pl.when(p != me)
        def _():
            mix_from(p - first, p).wait_recv()
    loop(first, first + owners, mix_in)

    project_all(1)

    def mix_out(p):
        @pl.when(p != me)
        def _():
            mix_from(p - first, p).wait_send()
    loop(first, first + owners, mix_out)

    def both_in(g):
        wait_left(g)
        sort(recv_l, 0, lh, 0, g)
        wait_right(first, g)
        sort(recv_r, first, rh, 0, g)
    loop(0, owners // GROUP, both_in)

    devices = width // rows
    for ic in range(cols // width):
        for jc in range(cols // width):
            for h in range(PER):
                spread(h, width, lax.dot_general(
                    lh[h, :, pl.ds(ic * width, width)],
                    rh[h, pl.ds(0, part), pl.ds(jc * width, width)],
                    (((0,), (0,)), ((), ())), preferred_element_type=F32))
            loop(0, devices, lambda q: gather(ic * devices + q, q, jc))

    recv_m[me] = send_m[me]

    def send_mix(k):
        p = lax.rem(me + k, n)
        mix_copy(p, p).start()
    loop(1, n, send_mix)
    wait_sent(1)

    def mix_in_all(k):
        p = lax.rem(me + k, n)
        mix_from(p, p).wait_recv()
    loop(1, n, mix_in_all)

    loop(0, pairs, lambda u: (finish(1, u, out_ref), None)[1])

    def mix_out_all(k):
        p = lax.rem(me + k, n)
        mix_from(p, p).wait_send()
    loop(1, n, mix_out_all)


def on_device(n, n_sub, pair_state, residue_mask, norm_gain, edge_weight, gate_weight, out_weight, mix_gain):
    rows, cols, chan = pair_state.shape
    hidden = out_weight.shape[1]
    owners = hidden // PER
    block = rows * PER
    width = min(cols, 32 * rows)
    vmem = pl.BlockSpec(memory_space=pltpu.VMEM)
    dma = pltpu.SemaphoreType.DMA
    flops = 2 * 2 * rows * cols * chan * (5 * hidden + chan) + 2 * 2 * PER * owners * rows * cols * cols
    return pl.pallas_call(
        functools.partial(kernel, n, n_sub),
        out_shape=jax.ShapeDtypeStruct(pair_state.shape, BF16),
        in_specs=[vmem, pl.BlockSpec(memory_space=pltpu.SMEM)] + [vmem] * 6,
        out_specs=vmem,
        scratch_shapes=[
            pltpu.VMEM((4 * hidden, chan), BF16),
            pltpu.VMEM((rows, cols, chan), BF16),
            pltpu.VMEM((owners, block, cols), BF16),
            pltpu.VMEM((owners, block, cols), BF16),
            pltpu.VMEM((owners, block, cols), BF16),
            pltpu.VMEM((n, block, cols), BF16),
            pltpu.VMEM((cols // LANES, GROUP * block, LANES), F32),
            pltpu.VMEM((PER, owners * rows, cols), BF16),
            pltpu.VMEM((PER, width, cols), BF16),
            pltpu.VMEM((width // LANES, PER * width, LANES), F32),
            pltpu.VMEM((n, block, cols), BF16),
            pltpu.VMEM((n, block, cols), BF16),
            dma((CHUNKS, owners)),
            dma((CHUNKS, n)),
            dma((n,)),
            dma((CHUNKS, owners)),
            dma((CHUNKS, n)),
            dma((n,)),
        ],
        compiler_params=pltpu.CompilerParams(
            collective_id=0, has_side_effects=True, vmem_limit_bytes=60 * 2**20),
        cost_estimate=pl.CostEstimate(
            flops=flops, bytes_accessed=4 * rows * cols * chan, transcendentals=0),
    )(
        pair_state, residue_mask, residue_mask.reshape(1, -1), norm_gain, edge_weight,
        gate_weight, out_weight, mix_gain[:, :, None],
    )


def solution(mesh):
    placed = (P(("grp", "dap", "sub"), None, None), P("grp"), P(), P(), P(), P(), P())
    n_sub = mesh.shape["sub"]
    return jax.shard_map(
        functools.partial(on_device, mesh.shape["dap"] * n_sub, n_sub),
        mesh=mesh,
        in_specs=placed,
        out_specs=P(("grp", "dap", "sub"), None, None),
        check_vma=False,
    )
```

```python
import functools

import jax
import jax.numpy as jnp
from jax import lax
from jax.experimental import pallas as pl
from jax.experimental.pallas import tpu as pltpu
from jax.sharding import PartitionSpec as P

PER = 8
GROUP = 4
LANES = 128
TILE = 16
F32 = jnp.float32
BF16 = jnp.bfloat16


def sigmoid(x):
    return 0.5 * jnp.tanh(0.5 * x) + 0.5


def kernel(
    n, n_sub,
    z_ref, mask_s, mask_v, ng_ref, ew_ref, gw_ref, ow_ref, mg_ref,
    out_ref,
    wt, gain, normed, send_l, send_r, recv_l, recv_r, stage, lh, rh, mf, send_m, recv_m,
    ss_l, ss_r, ss_m, rs_l, rs_r, rs_m,
):
    rows, cols, _ = z_ref.shape
    hidden = ow_ref.shape[1]
    owners = hidden // PER
    splits = n // owners
    block = rows * PER
    pairs = rows // 2
    part = owners * rows
    chunks = cols // LANES
    groups = owners // GROUP

    me = lax.axis_index("dap") * n_sub + lax.axis_index("sub")
    split = lax.div(me, owners)
    mine = lax.rem(me, owners)
    first = split * owners

    def device(p):
        return {"dap": lax.div(p, n_sub), "sub": lax.rem(p, n_sub)}

    def loop(lo, hi, body):
        lax.fori_loop(lo, hi, lambda i, c: (body(i), c)[1], 0)

    def turn(s, count):
        return jnp.where(2 * split >= splits, count - 1 - s, s)

    def lanes(v):
        return pl.ds(pl.multiple_of(v * LANES, LANES), LANES)

    barrier = pltpu.get_barrier_semaphore()
    loop(1, n, lambda k: pl.semaphore_signal(
        barrier, inc=1, device_id=device(lax.rem(me + k, n)),
        device_id_type=pl.DeviceIdType.MESH))

    def remote(src, dst, ssem, rsem, p):
        return pltpu.make_async_remote_copy(
            src_ref=src, dst_ref=dst, send_sem=ssem, recv_sem=rsem,
            device_id=device(p), device_id_type=pl.DeviceIdType.MESH)

    def left_copy(v, q, slot):
        return remote(send_l.at[q, v], recv_l.at[slot, v], ss_l.at[v, q], rs_l.at[v, slot], first + q)

    def right_copy(v, p, slot):
        return remote(
            send_r.at[lax.rem(p, owners), v], recv_r.at[slot, v], ss_r.at[v, p], rs_r.at[v, slot], p)

    def mix_copy(v, q, p, slot):
        return remote(send_m.at[q, v], recv_m.at[slot, v], ss_m.at[v, p], rs_m.at[v, slot], p)

    def away(k, s):
        return lax.rem(first + s * owners, n) + lax.rem(mine + k, owners)

    def start_left(v):
        recv_l[mine, v] = send_l[mine, v]
        loop(1, owners, lambda k: left_copy(v, lax.rem(mine + k, owners), mine).start())

    def start_right(v):
        recv_r[me, v] = send_r[mine, v]
        loop(1, owners, lambda k: right_copy(v, away(k, 0), me).start())

    def start_all(v, last):
        recv_l[mine, v] = send_l[mine, v]
        recv_r[me, v] = send_r[mine, v]

        def far(k):
            for s in range(1, splits):
                right_copy(v, away(k, s), me).start()

        def near(k):
            if not last:
                far(k)
            right_copy(v, away(k, 0), me).start()
            left_copy(v, lax.rem(mine + k, owners), mine).start()
        loop(1, owners, near)
        if last:
            loop(0, owners, far)
        else:
            far(0)

    def project(t, u, v, values):
        mean = jnp.mean(values, axis=-1, keepdims=True)
        centered = values - mean
        var = jnp.mean(centered * centered, axis=-1, keepdims=True)
        nr = (centered * lax.rsqrt(var + 1e-05) * ng_ref[pl.ds(t, 1), :]).astype(BF16)
        normed[pl.ds(2 * u, 2), lanes(v), :] = nr.reshape(2, LANES, -1)
        proj = lax.dot_general(wt[...], nr, (((1,), (1,)), ((), ())), preferred_element_type=F32)
        columns = mask_v[:, lanes(v)].astype(F32)
        mask = jnp.concatenate(
            [columns * mask_s[me * rows + 2 * u + i].astype(F32) for i in range(2)], axis=1)
        at = pl.ds(pl.multiple_of(u * TILE, TILE), TILE)
        for ref, k in ((send_l, 0), (send_r, 2)):
            side = sigmoid(proj[(k + 1) * hidden:(k + 2) * hidden]) * proj[k * hidden:(k + 1) * hidden] * mask
            both = jnp.concatenate(
                [side[:, i * LANES:(i + 1) * LANES].reshape(owners, PER, LANES) for i in range(2)], axis=1)
            ref[:, v, at, :] = both.astype(BF16)

    def finish(t, u, v, z):
        at = pl.ds(pl.multiple_of(u * TILE, TILE), TILE)
        if t == 0:
            got = recv_m[pl.ds(first, owners), v, at, :].astype(F32)
        else:
            got = recv_m[pl.ds(0, owners), v, at, :].astype(F32)
            for s in range(1, splits):
                got = got + recv_m[pl.ds(s * owners, owners), v, at, :].astype(F32)
        mixed = jnp.concatenate(
            [got[:, i * PER:(i + 1) * PER, :].reshape(hidden, LANES) for i in range(2)], axis=1)
        mean = jnp.mean(mixed, axis=0, keepdims=True)
        centered = mixed - mean
        var = jnp.mean(centered * centered, axis=0, keepdims=True)
        nm = (centered * lax.rsqrt(var + 1e-05) * gain[...]).astype(BF16)
        update = lax.dot_general(nm, ow_ref[t], (((0,), (0,)), ((), ())), preferred_element_type=F32)
        two = (pl.ds(2 * u, 2), lanes(v))
        gate = sigmoid(jnp.dot(
            normed[two[0], two[1], :].reshape(update.shape), gw_ref[t], preferred_element_type=F32))
        old = z[two[0], two[1], :].astype(F32).reshape(update.shape)
        new = (old + gate * update).astype(BF16)
        out_ref[two[0], two[1], :] = new.reshape(2, LANES, -1)
        return new.astype(F32)

    def sort(src, base, dst, g, v):
        stage[...] = src[pl.ds(base + g * GROUP, GROUP), v].astype(F32).reshape(stage.shape)
        for h in range(PER):
            dst[h, pl.ds(pl.multiple_of(g * GROUP * rows, TILE), GROUP * rows), lanes(v)] = stage[
                pl.ds(h, GROUP * rows, stride=PER), :].astype(BF16)

    def wait_left(g, v):
        def one(q):
            @pl.when(q != mine)
            def _():
                left_copy(v, q, q).wait_recv()
        loop(g * GROUP, (g + 1) * GROUP, one)

    def wait_right(base, g, v):
        def one(p):
            @pl.when(p != me)
            def _():
                right_copy(v, p, p).wait_recv()
        loop(base + g * GROUP, base + (g + 1) * GROUP, one)

    def prepare(t):
        wt[...] = ew_ref[t].astype(F32).T.astype(BF16)

    def prepare_gain(t):
        gain[...] = jnp.broadcast_to(mg_ref[pl.ds(t, 1), :], (hidden, hidden)).T[:, :1]

    def wait_sent(t):
        def one(k):
            for v in range(chunks):
                if t == 0:
                    for s in range(1, splits):
                        right_copy(v, away(k, s), me).wait_send()

                @pl.when(k > 0)
                def _():
                    right_copy(v, away(k, 0), me).wait_send()
                    left_copy(v, lax.rem(mine + k, owners), mine).wait_send()
        loop(0, owners, one)

    prepare(0)
    prepare_gain(0)
    for v in range(chunks):
        loop(0, pairs, lambda u: project(
            0, u, v, z_ref[pl.ds(2 * u, 2), lanes(v), :].astype(F32).reshape(2 * LANES, -1)))
        if v == 0:
            pl.semaphore_wait(barrier, n - 1)
        start_all(v, v == chunks - 1)
    prepare(1)

    def left_in(g):
        for v in range(chunks):
            wait_left(g, v)
            sort(recv_l, 0, lh, g, v)
    loop(0, groups, left_in)

    def right_in(i):
        g = turn(i, n // GROUP)
        for v in range(chunks):
            wait_right(0, g, v)
            sort(recv_r, 0, rh, g, v)

    done, sorted_by = 0, None
    for s in range(chunks):
        need = -(-(s + 1) * LANES // (GROUP * rows))
        if sorted_by is None and need >= (splits + 1) // 2 * groups:
            sorted_by = s
        loop(done, need, right_in)
        done = need
        v = turn(s, chunks)
        for h in range(PER):
            mf[pl.ds(h, part, stride=PER), :] = lax.dot_general(
                lh[h], rh[h, lanes(v), :], (((1,), (1,)), ((), ())), preferred_element_type=F32)

        def hand_back(k):
            q = lax.rem(mine + k, owners)
            send_m[q, v] = mf[pl.ds(pl.multiple_of(q * block, TILE), block), :].astype(BF16)

            @pl.when(k > 0)
            def _():
                mix_copy(v, q, first + q, me).start()
        loop(0, owners, hand_back)
        recv_m[me, v] = send_m[mine, v]
    wait_sent(0)

    for s in range(chunks):
        v = turn(s, chunks)

        def mix_in(k):
            p = away(k, 0)
            mix_copy(v, p - first, p, p).wait_recv()
        loop(1, owners, mix_in)
        loop(0, pairs, lambda u: project(1, u, v, finish(0, u, v, z_ref)))
        start_left(v)
        if s == sorted_by:
            start_right(turn(0, chunks))
    for s in range(1, chunks):
        start_right(turn(s, chunks))
    prepare_gain(1)

    def mix_out(k):
        for v in range(chunks):
            mix_copy(v, lax.rem(mine + k, owners), away(k, 0), me).wait_send()
    loop(1, owners, mix_out)

    for s in range(chunks):
        v = turn(s, chunks)

        def left_again(g):
            wait_left(g, v)
            sort(recv_l, 0, lh, g, v)
        loop(0, groups, left_again)
    for s in range(chunks):
        v = turn(s, chunks)

        def right_again(g):
            wait_right(first, g, v)
            sort(recv_r, first, rh, g, v)
        loop(0, groups, right_again)
        for h in range(PER):
            mf[pl.ds(h, cols, stride=PER), :] = lax.dot_general(
                lh[h], rh[h, pl.ds(0, part), lanes(v)], (((0,), (0,)), ((), ())),
                preferred_element_type=F32)

        def pack(p):
            send_m[p, v] = mf[pl.ds(pl.multiple_of(p * block, TILE), block), :].astype(BF16)

        def hand_out(k):
            for i in range(1, splits):
                p = away(k, i)
                pack(p)
                mix_copy(v, p, p, me).start()
            p = away(k, 0)
            pack(p)

            @pl.when(k > 0)
            def _():
                mix_copy(v, p, p, me).start()
        loop(0, owners, hand_out)
        recv_m[me, v] = send_m[me, v]
    wait_sent(1)

    for s in [chunks // 2] + [s for s in range(chunks) if s != chunks // 2]:
        v = turn(s, chunks)

        def mix_in_all(k):
            p = lax.rem(me + k, n)
            mix_copy(v, p, p, p).wait_recv()
        loop(1, n, mix_in_all)
        loop(0, pairs, lambda u: (finish(1, u, v, out_ref), None)[1])

    def mix_out_all(k):
        p = lax.rem(me + k, n)
        for v in range(chunks):
            mix_copy(v, p, p, me).wait_send()
    loop(1, n, mix_out_all)


def on_device(n, n_sub, pair_state, residue_mask, norm_gain, edge_weight, gate_weight, out_weight, mix_gain):
    rows, cols, chan = pair_state.shape
    hidden = out_weight.shape[1]
    owners = hidden // PER
    block = rows * PER
    chunks = cols // LANES
    vmem = pl.BlockSpec(memory_space=pltpu.VMEM)
    dma = pltpu.SemaphoreType.DMA
    flops = 2 * 2 * rows * cols * chan * (5 * hidden + chan) + 2 * 2 * PER * owners * rows * cols * cols
    return pl.pallas_call(
        functools.partial(kernel, n, n_sub),
        out_shape=jax.ShapeDtypeStruct(pair_state.shape, BF16),
        in_specs=[vmem, pl.BlockSpec(memory_space=pltpu.SMEM)] + [vmem] * 6,
        out_specs=vmem,
        scratch_shapes=[
            pltpu.VMEM((4 * hidden, chan), BF16),
            pltpu.VMEM((hidden, 1), F32),
            pltpu.VMEM((rows, cols, chan), BF16),
            pltpu.VMEM((owners, chunks, block, LANES), BF16),
            pltpu.VMEM((owners, chunks, block, LANES), BF16),
            pltpu.VMEM((owners, chunks, block, LANES), BF16),
            pltpu.VMEM((n, chunks, block, LANES), BF16),
            pltpu.VMEM((GROUP * block, LANES), F32),
            pltpu.VMEM((PER, owners * rows, cols), BF16),
            pltpu.VMEM((PER, n * rows, cols), BF16),
            pltpu.VMEM((PER * cols, LANES), F32),
            pltpu.VMEM((n, chunks, block, LANES), BF16),
            pltpu.VMEM((n, chunks, block, LANES), BF16),
            dma((chunks, owners)),
            dma((chunks, n)),
            dma((chunks, n)),
            dma((chunks, owners)),
            dma((chunks, n)),
            dma((chunks, n)),
        ],
        compiler_params=pltpu.CompilerParams(
            collective_id=0, has_side_effects=True, vmem_limit_bytes=60 * 2**20),
        cost_estimate=pl.CostEstimate(
            flops=flops, bytes_accessed=4 * rows * cols * chan, transcendentals=0),
    )(
        pair_state, residue_mask, residue_mask.reshape(1, -1), norm_gain, edge_weight,
        gate_weight, out_weight, mix_gain,
    )


def solution(mesh):
    placed = (P(("grp", "dap", "sub"), None, None), P("grp"), P(), P(), P(), P(), P())
    n_sub = mesh.shape["sub"]
    return jax.shard_map(
        functools.partial(on_device, mesh.shape["dap"] * n_sub, n_sub),
        mesh=mesh,
        in_specs=placed,
        out_specs=P(("grp", "dap", "sub"), None, None),
        check_vma=False,
    )
```

```python
import functools

import jax
import jax.numpy as jnp
from jax import lax
from jax.experimental import pallas as pl
from jax.experimental.pallas import tpu as pltpu
from jax.sharding import PartitionSpec as P

PER = 8
GROUP = 4
LANES = 128
TILE = 16
F32 = jnp.float32
BF16 = jnp.bfloat16


def sigmoid(x):
    return 0.5 * jnp.tanh(0.5 * x) + 0.5


def kernel(
    n, n_sub,
    z_in, mask_s, mask_in, ng_in, ew_in, gw_in, ow_in, mg_in,
    out_ref,
    z_ref, mask_v, ng_ref, ew_ref, gw_ref, ow_ref, mg_ref, in_sem,
    wt, gain, normed, send_l, send_r, recv_l, recv_r, recv_n, stage, lh, rh, mf, send_m, recv_m,
    ss_l, ss_r, ss_n, ss_m, rs_l, rs_r, rs_n, rs_m,
):
    rows, cols, _ = z_ref.shape
    hidden = ow_ref.shape[1]
    owners = hidden // PER
    splits = n // owners
    block = rows * PER
    pairs = rows // 2
    part = owners * rows
    chunks = cols // LANES
    groups = owners // GROUP

    me = lax.axis_index("dap") * n_sub + lax.axis_index("sub")
    split = lax.div(me, owners)
    mine = lax.rem(me, owners)
    first = split * owners

    def device(p):
        return {"dap": lax.div(p, n_sub), "sub": lax.rem(p, n_sub)}

    def loop(lo, hi, body):
        lax.fori_loop(lo, hi, lambda i, c: (body(i), c)[1], 0)

    def turn(s, count):
        return jnp.where(2 * split >= splits, count - 1 - s, s)

    def lanes(v):
        return pl.ds(pl.multiple_of(v * LANES, LANES), LANES)

    loads = [pltpu.make_async_copy(src, dst, in_sem.at[i]) for i, (src, dst) in enumerate((
        (ew_in, ew_ref), (z_in, z_ref), (mask_in, mask_v), (ng_in, ng_ref), (gw_in, gw_ref),
        (ow_in, ow_ref), (mg_in, mg_ref)))]
    for load in loads:
        load.start()

    barrier = pltpu.get_barrier_semaphore()
    loop(1, n, lambda k: pl.semaphore_signal(
        barrier, inc=1, device_id=device(lax.rem(me + k, n)),
        device_id_type=pl.DeviceIdType.MESH))

    def remote(src, dst, ssem, rsem, p):
        return pltpu.make_async_remote_copy(
            src_ref=src, dst_ref=dst, send_sem=ssem, recv_sem=rsem,
            device_id=device(p), device_id_type=pl.DeviceIdType.MESH)

    def left_copy(v, q, slot):
        return remote(send_l.at[q, v], recv_l.at[slot, v], ss_l.at[v, q], rs_l.at[v, slot], first + q)

    def right_copy(v, p, slot):
        return remote(
            send_r.at[lax.rem(p, owners), v], recv_r.at[slot, v], ss_r.at[v, p], rs_r.at[v, slot], p)

    def next_copy(v, q, slot):
        return remote(send_r.at[q, v], recv_n.at[slot, v], ss_n.at[v, q], rs_n.at[v, slot], first + q)

    def mix_copy(v, q, p, slot):
        return remote(send_m.at[q, v], recv_m.at[slot, v], ss_m.at[v, p], rs_m.at[v, slot], p)

    def away(k, s):
        return lax.rem(first + s * owners, n) + lax.rem(mine + k, owners)

    def start_left(v):
        recv_l[mine, v] = send_l[mine, v]
        loop(1, owners, lambda k: left_copy(v, lax.rem(mine + k, owners), mine).start())

    def start_right(v):
        recv_n[mine, v] = send_r[mine, v]
        loop(1, owners, lambda k: next_copy(v, lax.rem(mine + k, owners), mine).start())

    def start_all(v, last):
        recv_l[mine, v] = send_l[mine, v]
        recv_r[me, v] = send_r[mine, v]

        def far(k):
            for s in range(1, splits):
                right_copy(v, away(k, s), me).start()

        def near(k):
            if not last:
                far(k)
            right_copy(v, away(k, 0), me).start()
            left_copy(v, lax.rem(mine + k, owners), mine).start()
        loop(1, owners, near)
        if last:
            loop(0, owners, far)
        else:
            far(0)

    def project(t, u, v, values):
        mean = jnp.mean(values, axis=-1, keepdims=True)
        centered = values - mean
        var = jnp.mean(centered * centered, axis=-1, keepdims=True)
        nr = (centered * lax.rsqrt(var + 1e-05) * ng_ref[pl.ds(t, 1), :]).astype(BF16)
        normed[pl.ds(2 * u, 2), lanes(v), :] = nr.reshape(2, LANES, -1)
        proj = lax.dot_general(wt[...], nr, (((1,), (1,)), ((), ())), preferred_element_type=F32)
        columns = mask_v[lanes(v)].astype(F32).reshape(1, LANES)
        mask = jnp.concatenate(
            [columns * mask_s[me * rows + 2 * u + i].astype(F32) for i in range(2)], axis=1)
        at = pl.ds(pl.multiple_of(u * TILE, TILE), TILE)
        for ref, k in ((send_l, 0), (send_r, 2)):
            side = sigmoid(proj[(k + 1) * hidden:(k + 2) * hidden]) * proj[k * hidden:(k + 1) * hidden] * mask
            both = jnp.concatenate(
                [side[:, i * LANES:(i + 1) * LANES].reshape(owners, PER, LANES) for i in range(2)], axis=1)
            ref[:, v, at, :] = both.astype(BF16)

    def finish(t, u, v, z):
        at = pl.ds(pl.multiple_of(u * TILE, TILE), TILE)
        if t == 0:
            got = recv_m[pl.ds(first, owners), v, at, :].astype(F32)
        else:
            got = recv_m[pl.ds(0, owners), v, at, :].astype(F32)
            for s in range(1, splits):
                got = got + recv_m[pl.ds(s * owners, owners), v, at, :].astype(F32)
        mixed = jnp.concatenate(
            [got[:, i * PER:(i + 1) * PER, :].reshape(hidden, LANES) for i in range(2)], axis=1)
        mean = jnp.mean(mixed, axis=0, keepdims=True)
        centered = mixed - mean
        var = jnp.mean(centered * centered, axis=0, keepdims=True)
        nm = (centered * lax.rsqrt(var + 1e-05) * gain[...]).astype(BF16)
        update = lax.dot_general(nm, ow_ref[t], (((0,), (0,)), ((), ())), preferred_element_type=F32)
        two = (pl.ds(2 * u, 2), lanes(v))
        gate = sigmoid(jnp.dot(
            normed[two[0], two[1], :].reshape(update.shape), gw_ref[t], preferred_element_type=F32))
        old = z[two[0], two[1], :].astype(F32).reshape(update.shape)
        new = (old + gate * update).astype(BF16)
        out_ref[two[0], two[1], :] = new.reshape(2, LANES, -1)
        return new.astype(F32)

    def sort(src, base, dst, g, v):
        stage[...] = src[pl.ds(base + g * GROUP, GROUP), v].astype(F32).reshape(stage.shape)
        for h in range(PER):
            dst[h, pl.ds(pl.multiple_of(g * GROUP * rows, TILE), GROUP * rows), lanes(v)] = stage[
                pl.ds(h, GROUP * rows, stride=PER), :].astype(BF16)

    def wait_left(g, v):
        def one(q):
            @pl.when(q != mine)
            def _():
                left_copy(v, q, q).wait_recv()
        loop(g * GROUP, (g + 1) * GROUP, one)

    def wait_right(g, v):
        def one(p):
            @pl.when(p != me)
            def _():
                right_copy(v, p, p).wait_recv()
        loop(g * GROUP, (g + 1) * GROUP, one)

    def wait_next(g, v):
        def one(q):
            @pl.when(q != mine)
            def _():
                next_copy(v, q, q).wait_recv()
        loop(g * GROUP, (g + 1) * GROUP, one)

    def prepare(t):
        wt[...] = ew_ref[t].astype(F32).T.astype(BF16)

    def prepare_gain(t):
        gain[...] = jnp.broadcast_to(mg_ref[pl.ds(t, 1), :], (hidden, hidden)).T[:, :1]

    def wait_sent(t):
        def one(k):
            for v in range(chunks):
                if t == 0:
                    for s in range(1, splits):
                        right_copy(v, away(k, s), me).wait_send()

                @pl.when(k > 0)
                def _():
                    if t == 0:
                        right_copy(v, away(k, 0), me).wait_send()
                    else:
                        next_copy(v, lax.rem(mine + k, owners), mine).wait_send()
                    left_copy(v, lax.rem(mine + k, owners), mine).wait_send()
        loop(0, owners, one)

    for load in loads:
        load.wait()
    prepare(0)
    prepare_gain(0)
    for v in range(chunks):
        loop(0, pairs, lambda u: project(
            0, u, v, z_ref[pl.ds(2 * u, 2), lanes(v), :].astype(F32).reshape(2 * LANES, -1)))
        if v == 0:
            pl.semaphore_wait(barrier, n - 1)
        start_all(v, v == chunks - 1)
    prepare(1)

    def left_in(g):
        for v in range(chunks):
            wait_left(g, v)
            sort(recv_l, 0, lh, g, v)
    loop(0, groups, left_in)

    def right_in(i):
        g = turn(i, n // GROUP)
        for v in range(chunks):
            wait_right(g, v)
            sort(recv_r, 0, rh, g, v)

    done = 0
    for s in range(chunks):
        need = -(-(s + 1) * LANES // (GROUP * rows))
        loop(done, need, right_in)
        done = need
        v = turn(s, chunks)
        for h in range(PER):
            mf[pl.ds(h, part, stride=PER), :] = lax.dot_general(
                lh[h], rh[h, lanes(v), :], (((1,), (1,)), ((), ())), preferred_element_type=F32)

        def hand_back(k):
            q = lax.rem(mine + k, owners)
            send_m[q, v] = mf[pl.ds(pl.multiple_of(q * block, TILE), block), :].astype(BF16)

            @pl.when(k > 0)
            def _():
                mix_copy(v, q, first + q, me).start()
        loop(0, owners, hand_back)
        recv_m[me, v] = send_m[mine, v]
    wait_sent(0)

    for s in range(chunks):
        v = turn(s, chunks)

        def mix_in(k):
            p = away(k, 0)
            mix_copy(v, p - first, p, p).wait_recv()
        loop(1, owners, mix_in)
        loop(0, pairs, lambda u: project(1, u, v, finish(0, u, v, z_ref)))
        start_left(v)
        if s == 0:
            start_right(v)
    for s in range(1, chunks):
        start_right(turn(s, chunks))
    prepare_gain(1)

    def mix_out(k):
        for v in range(chunks):
            mix_copy(v, lax.rem(mine + k, owners), away(k, 0), me).wait_send()
    loop(1, owners, mix_out)

    def right_again(v):
        def one(g):
            wait_next(g, v)
            sort(recv_n, 0, rh, g, v)
        loop(0, groups, one)

    def pack(p, v):
        send_m[p, v] = mf[pl.ds(pl.multiple_of(p * block, TILE), block), :].astype(BF16)

    start = turn(0, chunks)
    done = 0
    for s in range(chunks):
        v = turn(s, chunks)

        def left_again(g):
            wait_left(g, v)
            sort(recv_l, 0, lh, g, v)
        loop(0, groups, left_again)
        if s == 0:
            right_again(start)
        for h in range(PER):
            mf[pl.ds(v * (LANES * PER) + h, LANES, stride=PER), :] = lax.dot_general(
                lh[h, :, lanes(v)], rh[h, pl.ds(0, part), lanes(start)], (((0,), (0,)), ((), ())),
                preferred_element_type=F32)
        ready = (s + 1) * LANES // rows

        def hand_some(k, lo=done, count=ready - done):
            p = turn(lo + lax.rem(mine + k, count), n)
            pack(p, start)

            @pl.when(p != me)
            def _():
                mix_copy(start, p, p, me).start()
        loop(0, ready - done, hand_some)
        done = ready
    recv_m[me, start] = send_m[me, start]
    for s in range(1, chunks):
        v = turn(s, chunks)
        right_again(v)
        for h in range(PER):
            mf[pl.ds(h, cols, stride=PER), :] = lax.dot_general(
                lh[h], rh[h, pl.ds(0, part), lanes(v)], (((0,), (0,)), ((), ())),
                preferred_element_type=F32)

        def hand_out(k):
            for i in range(1, splits):
                p = away(k, i)
                pack(p, v)
                mix_copy(v, p, p, me).start()
            p = away(k, 0)
            pack(p, v)

            @pl.when(k > 0)
            def _():
                mix_copy(v, p, p, me).start()
        loop(0, owners, hand_out)
        recv_m[me, v] = send_m[me, v]
    wait_sent(1)

    for s in [chunks // 2] + [s for s in range(chunks) if s != chunks // 2]:
        v = turn(s, chunks)

        def mix_in_all(k):
            p = lax.rem(me + k, n)
            mix_copy(v, p, p, p).wait_recv()
        loop(1, n, mix_in_all)
        loop(0, pairs, lambda u: (finish(1, u, v, out_ref), None)[1])

    def mix_out_all(k):
        p = lax.rem(me + k, n)
        for v in range(chunks):
            mix_copy(v, p, p, me).wait_send()
    loop(1, n, mix_out_all)


def on_device(n, n_sub, pair_state, residue_mask, norm_gain, edge_weight, gate_weight, out_weight, mix_gain):
    rows, cols, chan = pair_state.shape
    hidden = out_weight.shape[1]
    owners = hidden // PER
    block = rows * PER
    chunks = cols // LANES
    vmem = pl.BlockSpec(memory_space=pltpu.VMEM)
    hbm = pl.BlockSpec(memory_space=pltpu.HBM)
    dma = pltpu.SemaphoreType.DMA
    flops = 2 * 2 * rows * cols * chan * (5 * hidden + chan) + 2 * 2 * PER * owners * rows * cols * cols
    operands = (pair_state, residue_mask, norm_gain, edge_weight, gate_weight, out_weight, mix_gain)
    scratch = [pltpu.VMEM(x.shape, x.dtype) for x in operands] + [dma((len(operands),))] + [
        pltpu.VMEM((4 * hidden, chan), BF16),
        pltpu.VMEM((hidden, 1), F32),
        pltpu.VMEM((rows, cols, chan), BF16),
        pltpu.VMEM((owners, chunks, block, LANES), BF16),
        pltpu.VMEM((owners, chunks, block, LANES), BF16),
        pltpu.VMEM((owners, chunks, block, LANES), BF16),
        pltpu.VMEM((n, chunks, block, LANES), BF16),
        pltpu.VMEM((owners, chunks, block, LANES), BF16),
        pltpu.VMEM((GROUP * block, LANES), F32),
        pltpu.VMEM((PER, owners * rows, cols), BF16),
        pltpu.VMEM((PER, n * rows, cols), BF16),
        pltpu.VMEM((PER * cols, LANES), F32),
        pltpu.VMEM((n, chunks, block, LANES), BF16),
        pltpu.VMEM((n, chunks, block, LANES), BF16),
        dma((chunks, owners)),
        dma((chunks, n)),
        dma((chunks, owners)),
        dma((chunks, n)),
        dma((chunks, owners)),
        dma((chunks, n)),
        dma((chunks, owners)),
        dma((chunks, n)),
    ]
    return pl.pallas_call(
        functools.partial(kernel, n, n_sub),
        out_shape=jax.ShapeDtypeStruct(pair_state.shape, BF16),
        in_specs=[hbm, pl.BlockSpec(memory_space=pltpu.SMEM)] + [hbm] * 6,
        out_specs=vmem,
        scratch_shapes=scratch,
        compiler_params=pltpu.CompilerParams(
            collective_id=0, has_side_effects=True, vmem_limit_bytes=60 * 2**20),
        cost_estimate=pl.CostEstimate(
            flops=flops, bytes_accessed=4 * rows * cols * chan, transcendentals=0),
    )(
        pair_state, residue_mask, residue_mask, norm_gain, edge_weight,
        gate_weight, out_weight, mix_gain,
    )


def solution(mesh):
    placed = (P(("grp", "dap", "sub"), None, None), P("grp"), P(), P(), P(), P(), P())
    n_sub = mesh.shape["sub"]
    return jax.shard_map(
        functools.partial(on_device, mesh.shape["dap"] * n_sub, n_sub),
        mesh=mesh,
        in_specs=placed,
        out_specs=P(("grp", "dap", "sub"), None, None),
        check_vma=False,
    )
```

```python
import functools

import jax
import jax.numpy as jnp
from jax import lax
from jax.experimental import pallas as pl
from jax.experimental.pallas import tpu as pltpu
from jax.sharding import PartitionSpec as P

PER = 8
GROUP = 4
LANES = 128
TILE = 16
F32 = jnp.float32
BF16 = jnp.bfloat16


def sigmoid(x):
    return 0.5 * jnp.tanh(0.5 * x) + 0.5


def kernel(
    n, n_sub,
    z_ref, mask_s, mask_v, ng_ref, ew_ref, gw_ref, ow_ref, mg_ref,
    out_ref,
    wt, gain, normed, send_l, send_r, recv_l, recv_r, recv_n, stage, lh, rh, mf, send_m, recv_m,
    ss_l, ss_r, ss_n, ss_m, rs_l, rs_r, rs_n, rs_m,
):
    rows, cols, _ = z_ref.shape
    hidden = ow_ref.shape[1]
    owners = hidden // PER
    splits = n // owners
    block = rows * PER
    pairs = rows // 2
    part = owners * rows
    chunks = cols // LANES
    groups = owners // GROUP

    me = lax.axis_index("dap") * n_sub + lax.axis_index("sub")
    split = lax.div(me, owners)
    mine = lax.rem(me, owners)
    first = split * owners

    def device(p):
        return {"dap": lax.div(p, n_sub), "sub": lax.rem(p, n_sub)}

    def loop(lo, hi, body):
        lax.fori_loop(lo, hi, lambda i, c: (body(i), c)[1], 0)

    def turn(s, count):
        return jnp.where(2 * split >= splits, count - 1 - s, s)

    def lanes(v):
        return pl.ds(pl.multiple_of(v * LANES, LANES), LANES)

    barrier = pltpu.get_barrier_semaphore()
    loop(1, n, lambda k: pl.semaphore_signal(
        barrier, inc=1, device_id=device(lax.rem(me + k, n)),
        device_id_type=pl.DeviceIdType.MESH))

    def remote(src, dst, ssem, rsem, p):
        return pltpu.make_async_remote_copy(
            src_ref=src, dst_ref=dst, send_sem=ssem, recv_sem=rsem,
            device_id=device(p), device_id_type=pl.DeviceIdType.MESH)

    def left_copy(v, q, slot):
        return remote(send_l.at[q, v], recv_l.at[slot, v], ss_l.at[v, q], rs_l.at[v, slot], first + q)

    def right_copy(v, p, slot):
        return remote(
            send_r.at[lax.rem(p, owners), v], recv_r.at[slot, v], ss_r.at[v, p], rs_r.at[v, slot], p)

    def next_copy(v, q, slot):
        return remote(send_r.at[q, v], recv_n.at[slot, v], ss_n.at[v, q], rs_n.at[v, slot], first + q)

    def mix_copy(v, q, p, slot):
        return remote(send_m.at[q, v], recv_m.at[slot, v], ss_m.at[v, p], rs_m.at[v, slot], p)

    def away(k, s):
        return lax.rem(first + s * owners, n) + lax.rem(mine + k, owners)

    def start_left(v):
        recv_l[mine, v] = send_l[mine, v]
        loop(1, owners, lambda k: left_copy(v, lax.rem(mine + k, owners), mine).start())

    def start_right(v):
        recv_n[mine, v] = send_r[mine, v]
        loop(1, owners, lambda k: next_copy(v, lax.rem(mine + k, owners), mine).start())

    def start_all(v, last):
        recv_l[mine, v] = send_l[mine, v]
        recv_r[me, v] = send_r[mine, v]

        def far(k):
            for s in range(1, splits):
                right_copy(v, away(k, s), me).start()

        def near(k):
            left_copy(v, lax.rem(mine + k, owners), mine).start()
            right_copy(v, away(k, 0), me).start()
            if not last:
                far(k)
        loop(1, owners, near)
        if last:
            loop(0, owners, far)
        else:
            far(0)

    def project(t, u, v, values):
        mean = jnp.mean(values, axis=-1, keepdims=True)
        centered = values - mean
        var = jnp.mean(centered * centered, axis=-1, keepdims=True)
        nr = (centered * lax.rsqrt(var + 1e-05) * ng_ref[pl.ds(t, 1), :]).astype(BF16)
        normed[pl.ds(2 * u, 2), lanes(v), :] = nr.reshape(2, LANES, -1)
        proj = lax.dot_general(wt[...], nr, (((1,), (1,)), ((), ())), preferred_element_type=F32)
        columns = mask_v[lanes(v)].astype(F32).reshape(1, LANES)
        mask = jnp.concatenate(
            [columns * mask_s[me * rows + 2 * u + i].astype(F32) for i in range(2)], axis=1)
        at = pl.ds(pl.multiple_of(u * TILE, TILE), TILE)
        for ref, k in ((send_l, 0), (send_r, 2)):
            side = sigmoid(proj[(k + 1) * hidden:(k + 2) * hidden]) * proj[k * hidden:(k + 1) * hidden] * mask
            both = jnp.concatenate(
                [side[:, i * LANES:(i + 1) * LANES].reshape(owners, PER, LANES) for i in range(2)], axis=1)
            ref[:, v, at, :] = both.astype(BF16)

    def finish(t, u, v, z):
        at = pl.ds(pl.multiple_of(u * TILE, TILE), TILE)
        if t == 0:
            got = recv_m[pl.ds(first, owners), v, at, :].astype(F32)
        else:
            got = recv_m[pl.ds(0, owners), v, at, :].astype(F32)
            for s in range(1, splits):
                got = got + recv_m[pl.ds(s * owners, owners), v, at, :].astype(F32)
        mixed = jnp.concatenate(
            [got[:, i * PER:(i + 1) * PER, :].reshape(hidden, LANES) for i in range(2)], axis=1)
        mean = jnp.mean(mixed, axis=0, keepdims=True)
        centered = mixed - mean
        var = jnp.mean(centered * centered, axis=0, keepdims=True)
        nm = (centered * lax.rsqrt(var + 1e-05) * gain[...]).astype(BF16)
        update = lax.dot_general(nm, ow_ref[t], (((0,), (0,)), ((), ())), preferred_element_type=F32)
        two = (pl.ds(2 * u, 2), lanes(v))
        gate = sigmoid(jnp.dot(
            normed[two[0], two[1], :].reshape(update.shape), gw_ref[t], preferred_element_type=F32))
        old = z[two[0], two[1], :].astype(F32).reshape(update.shape)
        new = (old + gate * update).astype(BF16)
        out_ref[two[0], two[1], :] = new.reshape(2, LANES, -1)
        return new.astype(F32)

    def sort(src, base, dst, g, v):
        stage[...] = src[pl.ds(base + g * GROUP, GROUP), v].astype(F32).reshape(stage.shape)
        for h in range(PER):
            dst[h, pl.ds(pl.multiple_of(g * GROUP * rows, TILE), GROUP * rows), lanes(v)] = stage[
                pl.ds(h, GROUP * rows, stride=PER), :].astype(BF16)

    def wait_left(g, v):
        def one(q):
            @pl.when(q != mine)
            def _():
                left_copy(v, q, q).wait_recv()
        loop(g * GROUP, (g + 1) * GROUP, one)

    def wait_right(g, v):
        def one(p):
            @pl.when(p != me)
            def _():
                right_copy(v, p, p).wait_recv()
        loop(g * GROUP, (g + 1) * GROUP, one)

    def wait_next(g, v):
        def one(q):
            @pl.when(q != mine)
            def _():
                next_copy(v, q, q).wait_recv()
        loop(g * GROUP, (g + 1) * GROUP, one)

    def prepare(t):
        wt[...] = ew_ref[t].astype(F32).T.astype(BF16)

    def prepare_gain(t):
        gain[...] = jnp.broadcast_to(mg_ref[pl.ds(t, 1), :], (hidden, hidden)).T[:, :1]

    def wait_sent(t):
        def one(k):
            for v in range(chunks):
                if t == 0:
                    for s in range(1, splits):
                        right_copy(v, away(k, s), me).wait_send()

                @pl.when(k > 0)
                def _():
                    if t == 0:
                        right_copy(v, away(k, 0), me).wait_send()
                    else:
                        next_copy(v, lax.rem(mine + k, owners), mine).wait_send()
                    left_copy(v, lax.rem(mine + k, owners), mine).wait_send()
        loop(0, owners, one)

    prepare(0)
    prepare_gain(0)
    for v in range(chunks):
        loop(0, pairs, lambda u: project(
            0, u, v, z_ref[pl.ds(2 * u, 2), lanes(v), :].astype(F32).reshape(2 * LANES, -1)))
        if v == 0:
            pl.semaphore_wait(barrier, n - 1)
        start_all(v, v == chunks - 1)
    prepare(1)

    def left_in(g):
        for v in range(chunks):
            wait_left(g, v)
            sort(recv_l, 0, lh, g, v)
    loop(0, groups, left_in)

    def right_in(i):
        g = turn(i, n // GROUP)
        for v in range(chunks):
            wait_right(g, v)
            sort(recv_r, 0, rh, g, v)

    done = 0
    for s in range(chunks):
        need = -(-(s + 1) * LANES // (GROUP * rows))
        loop(done, need, right_in)
        done = need
        v = turn(s, chunks)
        for h in range(PER):
            mf[pl.ds(h, part, stride=PER), :] = lax.dot_general(
                lh[h], rh[h, lanes(v), :], (((1,), (1,)), ((), ())), preferred_element_type=F32)

        def hand_back(k):
            q = lax.rem(mine + k, owners)
            send_m[q, v] = mf[pl.ds(pl.multiple_of(q * block, TILE), block), :].astype(BF16)

            @pl.when(k > 0)
            def _():
                mix_copy(v, q, first + q, me).start()
        loop(0, owners, hand_back)
        recv_m[me, v] = send_m[mine, v]
    wait_sent(0)

    for s in range(chunks):
        v = turn(s, chunks)

        def mix_in(k):
            p = away(k, 0)
            mix_copy(v, p - first, p, p).wait_recv()
        loop(1, owners, mix_in)
        loop(0, pairs, lambda u: project(1, u, v, finish(0, u, v, z_ref)))
        start_left(v)
        if s == 0:
            start_right(v)
    for s in range(1, chunks):
        start_right(turn(s, chunks))
    prepare_gain(1)

    def mix_out(k):
        for v in range(chunks):
            mix_copy(v, lax.rem(mine + k, owners), away(k, 0), me).wait_send()
    loop(1, owners, mix_out)

    def right_again(v):
        def one(g):
            wait_next(g, v)
            sort(recv_n, 0, rh, g, v)
        loop(0, groups, one)

    def pack(p, v):
        send_m[p, v] = mf[pl.ds(pl.multiple_of(p * block, TILE), block), :].astype(BF16)

    start = turn(0, chunks)
    done = 0
    for s in range(chunks):
        v = turn(s, chunks)

        def left_again(g):
            wait_left(g, v)
            sort(recv_l, 0, lh, g, v)
        loop(0, groups, left_again)
        if s == 0:
            right_again(start)
        for h in range(PER):
            mf[pl.ds(v * (LANES * PER) + h, LANES, stride=PER), :] = lax.dot_general(
                lh[h, :, lanes(v)], rh[h, pl.ds(0, part), lanes(start)], (((0,), (0,)), ((), ())),
                preferred_element_type=F32)
        ready = (s + 1) * LANES // rows

        def hand_some(k, lo=done, count=ready - done):
            p = turn(lo + lax.rem(mine + k, count), n)
            pack(p, start)

            @pl.when(p != me)
            def _():
                mix_copy(start, p, p, me).start()
        loop(0, ready - done, hand_some)
        done = ready
    recv_m[me, start] = send_m[me, start]
    for s in range(1, chunks):
        v = turn(s, chunks)
        right_again(v)
        for h in range(PER):
            mf[pl.ds(h, cols, stride=PER), :] = lax.dot_general(
                lh[h], rh[h, pl.ds(0, part), lanes(v)], (((0,), (0,)), ((), ())),
                preferred_element_type=F32)

        def hand_out(k):
            for i in range(1, splits):
                p = away(k, i)
                pack(p, v)
                mix_copy(v, p, p, me).start()
            p = away(k, 0)
            pack(p, v)

            @pl.when(k > 0)
            def _():
                mix_copy(v, p, p, me).start()
        loop(0, owners, hand_out)
        recv_m[me, v] = send_m[me, v]
    wait_sent(1)

    for s in [chunks // 2] + [s for s in range(chunks) if s != chunks // 2]:
        v = turn(s, chunks)

        def mix_in_all(k):
            p = lax.rem(me + k, n)
            mix_copy(v, p, p, p).wait_recv()
        loop(1, n, mix_in_all)
        loop(0, pairs, lambda u: (finish(1, u, v, out_ref), None)[1])

    def mix_out_all(k):
        p = lax.rem(me + k, n)
        for v in range(chunks):
            mix_copy(v, p, p, me).wait_send()
    loop(1, n, mix_out_all)


def on_device(n, n_sub, pair_state, residue_mask, norm_gain, edge_weight, gate_weight, out_weight, mix_gain):
    rows, cols, chan = pair_state.shape
    hidden = out_weight.shape[1]
    owners = hidden // PER
    block = rows * PER
    chunks = cols // LANES
    vmem = pl.BlockSpec(memory_space=pltpu.VMEM)
    dma = pltpu.SemaphoreType.DMA
    flops = 2 * 2 * rows * cols * chan * (5 * hidden + chan) + 2 * 2 * PER * owners * rows * cols * cols
    return pl.pallas_call(
        functools.partial(kernel, n, n_sub),
        out_shape=jax.ShapeDtypeStruct(pair_state.shape, BF16),
        in_specs=[vmem, pl.BlockSpec(memory_space=pltpu.SMEM)] + [vmem] * 6,
        out_specs=vmem,
        scratch_shapes=[
            pltpu.VMEM((4 * hidden, chan), BF16),
            pltpu.VMEM((hidden, 1), F32),
            pltpu.VMEM((rows, cols, chan), BF16),
            pltpu.VMEM((owners, chunks, block, LANES), BF16),
            pltpu.VMEM((owners, chunks, block, LANES), BF16),
            pltpu.VMEM((owners, chunks, block, LANES), BF16),
            pltpu.VMEM((n, chunks, block, LANES), BF16),
            pltpu.VMEM((owners, chunks, block, LANES), BF16),
            pltpu.VMEM((GROUP * block, LANES), F32),
            pltpu.VMEM((PER, owners * rows, cols), BF16),
            pltpu.VMEM((PER, n * rows, cols), BF16),
            pltpu.VMEM((PER * cols, LANES), F32),
            pltpu.VMEM((n, chunks, block, LANES), BF16),
            pltpu.VMEM((n, chunks, block, LANES), BF16),
            dma((chunks, owners)),
            dma((chunks, n)),
            dma((chunks, owners)),
            dma((chunks, n)),
            dma((chunks, owners)),
            dma((chunks, n)),
            dma((chunks, owners)),
            dma((chunks, n)),
        ],
        compiler_params=pltpu.CompilerParams(
            collective_id=0, has_side_effects=True, vmem_limit_bytes=60 * 2**20),
        cost_estimate=pl.CostEstimate(
            flops=flops, bytes_accessed=4 * rows * cols * chan, transcendentals=0),
    )(
        pair_state, residue_mask, residue_mask, norm_gain, edge_weight,
        gate_weight, out_weight, mix_gain,
    )


def solution(mesh):
    placed = (P(("grp", "dap", "sub"), None, None), P("grp"), P(), P(), P(), P(), P())
    n_sub = mesh.shape["sub"]
    return jax.shard_map(
        functools.partial(on_device, mesh.shape["dap"] * n_sub, n_sub),
        mesh=mesh,
        in_specs=placed,
        out_specs=P(("grp", "dap", "sub"), None, None),
        check_vma=False,
    )
```
